32 devices in a mesh: vocab: 16 (over z, x, core), grp: 2 (over y).
Axes of the slice: x: 2, y: 2, z: 4, core: 2. Of those that a mesh axis runs over, the one named last changes fastest.
Arguments:
- hidden: bfloat16 [512, 4096], P('grp'), may hold values from -240 to 240
- head_weight: bfloat16 [4096, 32768], P('grp', 'vocab'), may hold values from -0.25 to 0.25
- cluster_weight: bfloat16 [4096, 3], replicated, may hold values from -0.5 to 0.5
- proj_one: bfloat16 [4096, 1024], P('vocab'), may hold values from -0.09375 to 0.09375
- proj_two: bfloat16 [4096, 256], P('vocab'), may hold values from -0.09375 to 0.09375
- proj_three: bfloat16 [4096, 64], P('vocab'), may hold values from -0.09375 to 0.09375
- tail_one: bfloat16 [1024, 65536], P('grp', 'vocab'), may hold values from -0.5 to 0.5
- tail_two: bfloat16 [256, 65536], P('grp', 'vocab'), may hold values from -1 to 1
- tail_three: bfloat16 [64, 65536], P('grp', 'vocab'), may hold values from -2 to 2
- targets: int32 [512], P('grp'), may hold values from 0 to 229375, as said below
- flags: int32 [512, 3], P('grp'), may hold values from 0 to 1, as said below
Outputs:
- target_logprob: float32 [512], P('grp')
- tail_entropy: float32 [512, 3], P('grp')
The draws below stay inside these ranges and needn't reach their ends.
Inputs may be any that keep to these rules, and one draw needn't show every extreme that they name: `targets`: a target at or beyond 32768 lies in tail (t - 32768) // 65536. flags[b, c] is 1 whenever the target of sequence b lies in tail c.
All inputs are finite; a program needn't handle non-finite values.
Results may differ from the reference program's by a relative error of at most 0.0092.
Values may be sent and summed in bfloat16 or wider, within the bound.
A program may use at most 128 MiB of HBM per device.

```python
import jax
import jax.numpy as jnp
from jax import lax

D = 4096
V_HEAD = 32768
TAIL = 65536
P1 = 1024
P2 = 256
P3 = 64
ROWS_GRP = 256
BATCH_SEQUENCES = 512


def draw_hidden(key, part):
    norm_random_key = jax.random.fold_in(jax.random.fold_in(key, 5), 0)
    values = jnp.clip(jax.random.normal(norm_random_key, (BATCH_SEQUENCES, D), jnp.float32), -6.0, 6.0)
    return values.astype(jnp.bfloat16)


def target_plan(key):
    base = jax.random.fold_in(key, 31)
    kkind, khead, ktail, kextra = jax.random.split(base, 4)
    kind = jax.random.randint(kkind, (BATCH_SEQUENCES,), 0, 5)
    head_word = jax.random.randint(khead, (BATCH_SEQUENCES,), 0, V_HEAD)
    tail_word = jax.random.randint(ktail, (BATCH_SEQUENCES,), 0, TAIL)
    chosen = jnp.where(kind < 2, head_word, V_HEAD + (kind - 2) * TAIL + tail_word).astype(jnp.int32)
    extra = jax.random.randint(kextra, (BATCH_SEQUENCES, 3), 0, 2)
    owned = (kind[:, None] - 2 == jnp.arange(3)[None, :]).astype(jnp.int32)
    return (chosen, jnp.maximum(extra, owned).astype(jnp.int32))


def draw_targets(key, part):
    return target_plan(key)[0]


def draw_flags(key, part):
    return target_plan(key)[1]


def steps_of(key, extent, cuts, smallest, high):
    def one(dim, blocks):
        heights = jax.random.uniform(jax.random.fold_in(jax.random.fold_in(key, 6), dim), (blocks,), jnp.float32, smallest / len(cuts), high / len(cuts))
        return jnp.repeat(jnp.exp(heights), extent[dim] // blocks).reshape((-1,) + (1,) * (len(extent) - dim - 1))

    level = one(*cuts[0])
    for cut in cuts[1:]:
        level = level * one(*cut)
    return level


def normal_values(key, dims, width, most, cuts=(), held_as=jnp.bfloat16):
    level = steps_of(key, dims, cuts, -0.22, 0.18) if cuts else 1.0
    entries = jax.random.normal(key, dims, jnp.float32) * width * level
    return jnp.minimum(jnp.maximum(entries, -most), most).astype(held_as)


def setup_inputs(seed: int = 0) -> dict:
    key_list = jax.random.split(jax.random.key(seed), 12)
    return {
        "hidden": draw_hidden(jax.random.fold_in(key_list[11], 71), 0),
        "head_weight": normal_values(key_list[1], (D, V_HEAD), (D // 9) ** -0.5, 0.25, ((0, 2), (1, 16))),
        "cluster_weight": normal_values(key_list[2], (D, 3), (D // 36) ** -0.5, 0.5),
        "proj_one": normal_values(key_list[3], (D, P1), D ** -0.5, 0.09375, ((0, 16),)),
        "proj_two": normal_values(key_list[4], (D, P2), D ** -0.5, 0.09375, ((0, 16),)),
        "proj_three": normal_values(key_list[5], (D, P3), D ** -0.5, 0.09375, ((0, 16),)),
        "tail_one": normal_values(key_list[6], (P1, TAIL), (P1 // 9) ** -0.5, 0.5, ((0, 2), (1, 16))),
        "tail_two": normal_values(key_list[7], (P2, TAIL), (P2 // 9) ** -0.5, 1.0, ((0, 2), (1, 16))),
        "tail_three": normal_values(key_list[8], (P3, TAIL), (max(P3 // 9, 1)) ** -0.5, 2.0, ((0, 2), (1, 16))),
        "targets": draw_targets(jax.random.fold_in(key_list[11], 71), 0),
        "flags": draw_flags(jax.random.fold_in(key_list[11], 71), 0),
    }


def tail_stats(projected, tail_weight):
    logits = jnp.dot(projected, tail_weight, preferred_element_type=jnp.float32)
    top = jnp.max(logits, axis=1)
    expo = jnp.exp(logits - top[:, None])
    total = jnp.sum(expo, axis=1)
    lse = top + jnp.log(total)
    mean = jnp.sum(expo * logits, axis=1) / total
    return logits, lse, mean


def reference(hidden, head_weight, cluster_weight, proj_one, proj_two, proj_three, tail_one, tail_two, tail_three, targets, flags):
    blocks = BATCH_SEQUENCES // ROWS_GRP
    hid_blocks = hidden.reshape(blocks, ROWS_GRP, D)
    tgt_blocks = targets.reshape(blocks, ROWS_GRP)
    flag_blocks = flags.reshape(blocks, ROWS_GRP, 3)
    projections = (proj_one, proj_two, proj_three)
    tails = (tail_one, tail_two, tail_three)

    def one_block(items):
        rows, tgt, flg = items
        head_logits = jnp.dot(rows, head_weight, preferred_element_type=jnp.float32)
        cluster_score_logits = jnp.dot(rows, cluster_weight, preferred_element_type=jnp.float32)
        top = jnp.maximum(jnp.max(head_logits, axis=1), jnp.max(cluster_score_logits, axis=1))
        total = jnp.sum(jnp.exp(head_logits - top[:, None]), axis=1) + jnp.sum(jnp.exp(cluster_score_logits - top[:, None]), axis=1)
        head_lse = top + jnp.log(total)
        relative = tgt - V_HEAD
        cluster = relative // TAIL
        word = relative - cluster * TAIL
        head_pick = jnp.take_along_axis(head_logits, jnp.clip(tgt, 0, V_HEAD - 1).astype(jnp.int32)[:, None], axis=1)[:, 0]
        lse_list = []
        mean_list = []
        tail_pick = jnp.zeros(tgt.shape, jnp.float32)
        for index in range(3):
            projected = jnp.dot(rows, projections[index], preferred_element_type=jnp.float32).astype(jnp.bfloat16)
            logits, lse, mean = tail_stats(projected, tails[index])
            lse_list.append(lse)
            mean_list.append(mean)
            picked = jnp.take_along_axis(logits, jnp.clip(word, 0, TAIL - 1).astype(jnp.int32)[:, None], axis=1)[:, 0]
            tail_pick = tail_pick + jnp.where(cluster == index, picked - lse + cluster_score_logits[:, index], 0.0)
        tail_lse = jnp.stack(lse_list, axis=1)
        tail_mean = jnp.stack(mean_list, axis=1)
        entropy = flg.astype(jnp.float32) * (tail_lse - tail_mean)
        logprob = jnp.where(tgt < V_HEAD, head_pick, tail_pick) - head_lse
        return logprob, entropy

    logprob, entropy = lax.map(one_block, (hid_blocks, tgt_blocks, flag_blocks))
    return logprob.reshape(BATCH_SEQUENCES), entropy.reshape(BATCH_SEQUENCES, 3)
```

```python
import functools

import jax
import jax.numpy as jnp
from jax import lax
from jax.experimental import pallas as pl
from jax.experimental.pallas import tpu as pltpu
from jax.sharding import PartitionSpec as P

MESH = pl.DeviceIdType.MESH
VMEM = pl.BlockSpec(memory_space=pltpu.VMEM)
F32 = jnp.float32
BF16 = jnp.bfloat16


def greet(nv, n, members, v, g):
    barrier = pltpu.get_barrier_semaphore()

    def one(d, carry):
        pl.semaphore_signal(barrier, inc=1, device_id=(peer(v, d, members), g), device_id_type=MESH)
        return carry

    lax.fori_loop(1, members, one, 0)
    for s in range(1, n):
        pl.semaphore_signal(barrier, inc=1, device_id=(v, lax.rem(g + s, n)), device_id_type=MESH)
    pl.semaphore_wait(barrier, members - 1 + n - 1)


def peer(v, d, members):
    base = (v // members) * members
    return base + lax.rem(v - base + d, members)


def spread(src, buf, slot, v, g, members, send, recv, landed):
    def copy(d):
        return pltpu.make_async_remote_copy(
            src_ref=src,
            dst_ref=landed(slot),
            send_sem=send.at[d],
            recv_sem=recv.at[d],
            device_id=(peer(v, d, members), g),
            device_id_type=MESH,
        )

    def arrival(d):
        from_slot = lax.rem(slot - d + members, members)
        return pltpu.make_async_remote_copy(
            src_ref=src,
            dst_ref=landed(from_slot),
            send_sem=send.at[d],
            recv_sem=recv.at[d],
            device_id=(peer(v, d, members), g),
            device_id_type=MESH,
        )

    def start(d, carry):
        copy(d).start()
        return carry

    def finish(d, carry):
        copy(d).wait_send()
        arrival(d).wait_recv()
        return carry

    lax.fori_loop(1, members, start, 0)
    return lambda: lax.fori_loop(1, members, finish, 0)


def across(src, dst, s, v, g, n, sign, send, recv):
    return pltpu.make_async_remote_copy(
        src_ref=src,
        dst_ref=dst,
        send_sem=send.at[s],
        recv_sem=recv.at[s],
        device_id=(v, lax.rem(g + sign * s + n, n)),
        device_id_type=MESH,
    )


def hidden_kernel(n, nv, members, piece_ref, out_ref, buf, ysend, yrecv, send, recv):
    v, g = lax.axis_index("vocab"), lax.axis_index("grp")
    slot = lax.rem(v, members)
    greet(nv, n, members, v, g)
    crossing = [
        across(piece_ref.at[s - 1], buf.at[s - 1, slot], s, v, g, n, 1, ysend, yrecv)
        for s in range(1, n)
    ]
    for copy in crossing:
        copy.start()
    waits = []
    for s in range(1, n):
        crossing[s - 1].wait_recv()
        waits.append(
            spread(
                buf.at[s - 1, slot], buf, slot, v, g, members,
                send.at[s - 1], recv.at[s - 1], lambda i, s=s: buf.at[s - 1, i],
            )
        )
    for s in range(1, n):
        crossing[s - 1].wait_send()
        waits[s - 1]()
    out_ref[...] = buf[...]


def exchange_hidden(pieces, n, nv, members):
    shape = (n - 1, members) + pieces.shape[1:]
    return pl.pallas_call(
        functools.partial(hidden_kernel, n, nv, members),
        out_shape=jax.ShapeDtypeStruct(shape, pieces.dtype),
        in_specs=[VMEM],
        out_specs=VMEM,
        scratch_shapes=[
            pltpu.VMEM(shape, pieces.dtype),
            pltpu.SemaphoreType.DMA((n,)),
            pltpu.SemaphoreType.DMA((n,)),
            pltpu.SemaphoreType.DMA((n - 1, members)),
            pltpu.SemaphoreType.DMA((n - 1, members)),
        ],
        compiler_params=pltpu.CompilerParams(
            collective_id=1, has_side_effects=True, vmem_limit_bytes=40 << 20
        ),
        name="hidden_exchange",
    )(pieces)


def proj_kernel(n, nv, part_ref, out_ref, mail, buf, ysend, yrecv, rsend, rrecv, send, recv):
    v, g = lax.axis_index("vocab"), lax.axis_index("grp")
    greet(nv, n, nv, v, g)

    def give(d):
        return pltpu.make_async_remote_copy(
            src_ref=part_ref.at[lax.rem(v + d, nv)],
            dst_ref=mail.at[d],
            send_sem=rsend.at[d],
            recv_sem=rrecv.at[d],
            device_id=(lax.rem(v + d, nv), g),
            device_id_type=MESH,
        )

    def start(d, carry):
        give(d).start()
        return carry

    lax.fori_loop(1, nv, start, 0)

    def add(d, total):
        give(d).wait()
        return total + mail[d].astype(F32)

    total = lax.fori_loop(1, nv, add, part_ref[v].astype(F32))
    buf[0, v] = total.astype(BF16)
    crossing = [across(buf.at[0, v], buf.at[s, v], s, v, g, n, 1, ysend, yrecv) for s in range(1, n)]
    for copy in crossing:
        copy.start()
    waits = []
    for s in range(n):
        if s:
            crossing[s - 1].wait_recv()
        waits.append(
            spread(
                buf.at[s, v], buf, v, v, g, nv, send.at[s], recv.at[s],
                lambda i, s=s: buf.at[s, i],
            )
        )
    for copy in crossing:
        copy.wait_send()
    for wait in waits:
        wait()
    out_ref[...] = buf[...]


def sum_projections(parts, n, nv):
    shape = (n,) + parts.shape
    return pl.pallas_call(
        functools.partial(proj_kernel, n, nv),
        out_shape=jax.ShapeDtypeStruct(shape, BF16),
        in_specs=[VMEM],
        out_specs=VMEM,
        scratch_shapes=[
            pltpu.VMEM(parts.shape, BF16),
            pltpu.VMEM(shape, BF16),
            pltpu.SemaphoreType.DMA((n,)),
            pltpu.SemaphoreType.DMA((n,)),
            pltpu.SemaphoreType.DMA((nv,)),
            pltpu.SemaphoreType.DMA((nv,)),
            pltpu.SemaphoreType.DMA((n, nv)),
            pltpu.SemaphoreType.DMA((n, nv)),
        ],
        compiler_params=pltpu.CompilerParams(
            collective_id=2, has_side_effects=True, vmem_limit_bytes=40 << 20
        ),
        name="projection_sum",
    )(parts)


def merge(blocks):
    rows = []
    for c in range(4):
        m, s, w, p = (blocks[:, 4 * c + i, :] for i in range(4))
        top = jnp.max(m, axis=0, keepdims=True)
        scale = jnp.exp(m - top)
        rows += [
            top,
            jnp.sum(s * scale, axis=0, keepdims=True),
            jnp.sum(w * scale, axis=0, keepdims=True),
            jnp.sum(p, axis=0, keepdims=True),
        ]
    return rows


def final_kernel(n, nv, v_head, tail, tail_ref, head_ref, clus_ref, tgt_ref, flag_ref, out_ref,
                 mail, buf, ysend, yrecv, send, recv):
    v, g = lax.axis_index("vocab"), lax.axis_index("grp")
    greet(nv, n, nv, v, g)
    crossing = [
        across(tail_ref.at[s], mail.at[s], s, v, g, n, -1, ysend, yrecv) for s in range(1, n)
    ]
    for copy in crossing:
        copy.start()
    mail[0] = tail_ref[0]
    for copy in crossing:
        copy.wait()
    rows = merge(mail[...])
    buf[v] = jnp.concatenate(rows[:12] + [head_ref[...]], axis=0)
    spread(buf.at[v], buf, v, v, g, nv, send, recv, lambda i: buf.at[i])()
    rows = merge(buf[...])
    clus = clus_ref[...]
    targets = tgt_ref[...]
    head_max, head_sum, _, picked = rows[12:]
    for c in range(3):
        picked = picked + rows[4 * c + 3]
    top = jnp.maximum(head_max, jnp.max(clus, axis=0, keepdims=True))
    total = head_sum * jnp.exp(head_max - top) + jnp.sum(jnp.exp(clus - top), axis=0, keepdims=True)
    head_lse = top + jnp.log(total)
    term = jnp.zeros_like(head_lse)
    out = []
    for c in range(3):
        lse = rows[4 * c] + jnp.log(rows[4 * c + 1])
        mean = rows[4 * c + 2] / rows[4 * c + 1]
        out.append(flag_ref[c : c + 1, :] * (lse - mean))
        low = v_head + c * tail
        inside = jnp.logical_and(targets >= low, targets < low + tail)
        term = term + jnp.where(inside, clus[c : c + 1, :] - lse, 0.0)
    out_ref[...] = jnp.concatenate([picked + term - head_lse] + out, axis=0)


def finish(tails, head, clus, targets, flags, n, nv, v_head, tail):
    rows = head.shape[1]
    return pl.pallas_call(
        functools.partial(final_kernel, n, nv, v_head, tail),
        out_shape=jax.ShapeDtypeStruct((4, rows), F32),
        in_specs=[VMEM] * 5,
        out_specs=VMEM,
        scratch_shapes=[
            pltpu.VMEM((n, 16, rows), F32),
            pltpu.VMEM((nv, 16, rows), F32),
            pltpu.SemaphoreType.DMA((n,)),
            pltpu.SemaphoreType.DMA((n,)),
            pltpu.SemaphoreType.DMA((nv,)),
            pltpu.SemaphoreType.DMA((nv,)),
        ],
        compiler_params=pltpu.CompilerParams(
            collective_id=3, has_side_effects=True, vmem_limit_bytes=40 << 20
        ),
        name="totals",
    )(tails, head, clus, targets, flags)


def stats_kernel(parts, tile, *refs):
    xs, ws = refs[:parts], refs[parts : 2 * parts]
    tgt_ref, out_ref, acc = refs[2 * parts :]
    step = pl.program_id(0)

    @pl.when(step == 0)
    def _():
        acc[:, 0:1] = jnp.full((acc.shape[0], 1), -jnp.inf, F32)
        acc[:, 1:] = jnp.zeros((acc.shape[0], acc.shape[1] - 1), F32)

    logits = jnp.dot(xs[0][...], ws[0][...], preferred_element_type=F32)
    for x, w in zip(xs[1:], ws[1:]):
        logits += jnp.dot(x[...], w[...], preferred_element_type=F32)
    before = acc[:, 0:1]
    top = jnp.maximum(before, jnp.max(logits, axis=1, keepdims=True))
    scale = jnp.exp(before - top)
    expo = jnp.exp(logits - top)
    ids = lax.broadcasted_iota(jnp.int32, logits.shape, 1) + step * tile
    acc[:, 0:1] = top
    acc[:, 1:2] = acc[:, 1:2] * scale + jnp.sum(expo, axis=1, keepdims=True)
    acc[:, 2:3] = acc[:, 2:3] * scale + jnp.sum(expo * logits, axis=1, keepdims=True)
    acc[:, 3:4] += jnp.sum(jnp.where(ids == tgt_ref[...], logits, 0.0), axis=1, keepdims=True)

    @pl.when(step == pl.num_programs(0) - 1)
    def _():
        out_ref[...] = acc[...].T[:8]


def softmax_stats(xs, ws, targets):
    rows, words = xs[0].shape[0], ws[0].shape[1]
    tile = min(512, words)
    depth = sum(w.shape[0] for w in ws)
    return pl.pallas_call(
        functools.partial(stats_kernel, len(xs), tile),
        grid=(words // tile,),
        out_shape=jax.ShapeDtypeStruct((8, rows), F32),
        in_specs=[pl.BlockSpec(x.shape, lambda i: (0, 0)) for x in xs]
        + [pl.BlockSpec((w.shape[0], tile), lambda i: (0, i)) for w in ws]
        + [pl.BlockSpec((rows, 1), lambda i: (0, 0))],
        out_specs=pl.BlockSpec((8, rows), lambda i: (0, 0)),
        scratch_shapes=[pltpu.VMEM((rows, 128), F32)],
        compiler_params=pltpu.CompilerParams(vmem_limit_bytes=40 << 20),
        cost_estimate=pl.CostEstimate(
            flops=2 * rows * words * depth + 20 * rows * words,
            bytes_accessed=2 * depth * (rows + words),
            transcendentals=rows * words,
        ),
        name="softmax_stats",
    )(*xs, *ws, targets)


def shards(
    n, nv, hidden, head_weight, cluster_weight, proj_one, proj_two, proj_three,
    tail_one, tail_two, tail_three, targets, flags,
):
    v, g = lax.axis_index("vocab"), lax.axis_index("grp")
    rows, width = hidden.shape
    depth = width // n
    head_cols, tail_cols = head_weight.shape[1], tail_one.shape[1]
    v_head, tail = head_cols * nv, tail_cols * nv
    share = tail_cols // n
    members = 4 if nv % 4 == 0 else 1

    def shift(value, s):
        return lax.ppermute(value, "grp", [(i, (i + s) % n) for i in range(n)])

    def columns(value, index, size):
        return lax.dynamic_slice_in_dim(value, index * size, size, 1)

    quarter = rows // members
    mine = lax.dynamic_slice_in_dim(hidden, lax.rem(v, members) * quarter, quarter, 0)
    pieces = jnp.stack([columns(mine, (g + s) % n, depth) for s in range(1, n)])
    others = exchange_hidden(pieces, n, nv, members).reshape(n - 1, rows, depth)

    two = [columns(tail_two, g, share)] + [shift(columns(tail_two, (g + s) % n, share), s) for s in range(1, n)]
    three = [columns(tail_three, g, share)] + [shift(columns(tail_three, (g + s) % n, share), s) for s in range(1, n)]
    one_src, others = lax.optimization_barrier((tail_one, others))
    one = [columns(one_src, g, share)] + [shift(columns(one_src, (g + s) % n, share), s) for s in range(1, n)]
    all_targets = jnp.concatenate([targets] + [shift(targets, s) for s in range(1, n)])

    sent = [jnp.dot(others[s - 1], head_weight, preferred_element_type=F32).astype(BF16) for s in range(1, n)]
    features = columns(hidden, v, proj_one.shape[0])
    parts = jnp.concatenate(
        [jnp.dot(features, w, preferred_element_type=F32).astype(BF16) for w in (proj_one, proj_two, proj_three)],
        axis=1,
    )
    sent, parts = lax.optimization_barrier((sent, parts))
    arrived = [shift(sent[s - 1], -s) for s in range(1, n)]
    own = jnp.dot(columns(hidden, g, depth), head_weight, preferred_element_type=F32)
    projected = sum_projections(parts.reshape(nv, rows // nv, -1), n, nv).reshape(n * rows, -1)

    def ordered(value, weight):
        size = weight.shape[0]
        return [columns(value, (g - s + n) % n, size) for s in range(n)]

    p1, p2 = proj_one.shape[1], proj_two.shape[1]
    proj = (projected[:, :p1], projected[:, p1 : p1 + p2], projected[:, p1 + p2 :])
    relative = all_targets - v_head
    cluster = relative // tail
    local = relative - cluster * tail - (v * tail_cols + g * share)
    marks = [jnp.where(cluster == c, local, -1)[:, None] for c in range(3)]

    def joined(value, weights, mark):
        x = jnp.concatenate(ordered(value, weights[0]), axis=1)
        return softmax_stats([x], [jnp.concatenate(weights, axis=0)], mark)

    stats_two = joined(proj[1], two, marks[1])
    stats_three = joined(proj[2], three, marks[2])
    stats_one = softmax_stats(ordered(proj[0], tail_one), one, marks[0])
    totals = jnp.concatenate([stats_one[:4], stats_two[:4], stats_three[:4], jnp.zeros((4, n * rows), F32)])
    totals = jnp.transpose(totals.reshape(16, n, rows), (1, 0, 2))

    logits = own
    for value in arrived:
        logits = logits + value.astype(F32)
    head_max = jnp.max(logits, axis=1)
    head_sum = jnp.sum(jnp.exp(logits - head_max[:, None]), axis=1)
    ids = v * head_cols + lax.broadcasted_iota(jnp.int32, logits.shape, 1)
    head_pick = jnp.sum(jnp.where(ids == targets[:, None], logits, 0.0), axis=1)
    head = jnp.stack([head_max, head_sum, jnp.zeros_like(head_sum), head_pick])
    clus = jnp.dot(hidden, cluster_weight, preferred_element_type=F32)

    out = finish(totals, head, clus.T, targets[None, :], flags.astype(F32).T, n, nv, v_head, tail)
    return out[0], out[1:].T


def solution(mesh):
    n, nv = mesh.shape["grp"], mesh.shape["vocab"]
    return jax.shard_map(
        functools.partial(shards, n, nv),
        mesh=mesh,
        in_specs=(
            P("grp", None),
            P("grp", "vocab"),
            P(),
            P("vocab", None),
            P("vocab", None),
            P("vocab", None),
            P("grp", "vocab"),
            P("grp", "vocab"),
            P("grp", "vocab"),
            P("grp"),
            P("grp", None),
        ),
        out_specs=(P("grp"), P("grp", None)),
        check_vma=False,
    )
```

```python
import functools

import jax
import jax.numpy as jnp
from jax import lax
from jax.experimental import pallas as pl
from jax.experimental.pallas import tpu as pltpu
from jax.sharding import PartitionSpec as P

MESH = pl.DeviceIdType.MESH
VMEM = pl.BlockSpec(memory_space=pltpu.VMEM)
F32 = jnp.float32
BF16 = jnp.bfloat16


def greet(nv, n, members, v, g):
    barrier = pltpu.get_barrier_semaphore()

    def one(d, carry):
        pl.semaphore_signal(barrier, inc=1, device_id=(peer(v, d, members), g), device_id_type=MESH)
        return carry

    lax.fori_loop(1, members, one, 0)
    for s in range(1, n):
        pl.semaphore_signal(barrier, inc=1, device_id=(v, lax.rem(g + s, n)), device_id_type=MESH)
    pl.semaphore_wait(barrier, members - 1 + n - 1)


def peer(v, d, members):
    base = (v // members) * members
    return base + lax.rem(v - base + d, members)


def spread(src, buf, slot, v, g, members, send, recv, landed):
    def copy(d):
        return pltpu.make_async_remote_copy(
            src_ref=src,
            dst_ref=landed(slot),
            send_sem=send.at[d],
            recv_sem=recv.at[d],
            device_id=(peer(v, d, members), g),
            device_id_type=MESH,
        )

    def arrival(d):
        from_slot = lax.rem(slot - d + members, members)
        return pltpu.make_async_remote_copy(
            src_ref=src,
            dst_ref=landed(from_slot),
            send_sem=send.at[d],
            recv_sem=recv.at[d],
            device_id=(peer(v, d, members), g),
            device_id_type=MESH,
        )

    def start(d, carry):
        copy(d).start()
        return carry

    def finish(d, carry):
        copy(d).wait_send()
        arrival(d).wait_recv()
        return carry

    lax.fori_loop(1, members, start, 0)
    return lambda: lax.fori_loop(1, members, finish, 0)


def across(src, dst, s, v, g, n, sign, send, recv):
    return pltpu.make_async_remote_copy(
        src_ref=src,
        dst_ref=dst,
        send_sem=send.at[s],
        recv_sem=recv.at[s],
        device_id=(v, lax.rem(g + sign * s + n, n)),
        device_id_type=MESH,
    )


def front_kernel(n, nv, members, piece_ref, part_ref, hid_ref, out_ref, hid, mail, buf,
                 ysend, yrecv, rsend, rrecv, send, recv):
    v, g = lax.axis_index("vocab"), lax.axis_index("grp")
    slot = lax.rem(v, members)
    greet(nv, n, nv, v, g)

    def give(d):
        return pltpu.make_async_remote_copy(
            src_ref=part_ref.at[lax.rem(v + d, nv)],
            dst_ref=mail.at[d],
            send_sem=rsend.at[d],
            recv_sem=rrecv.at[d],
            device_id=(lax.rem(v + d, nv), g),
            device_id_type=MESH,
        )

    def start(d, carry):
        give(d).start()
        return carry

    lax.fori_loop(1, nv, start, 0)
    waits = [
        spread(
            piece_ref.at[s - 1], hid, slot, v, g, members,
            send.at[s - 1], recv.at[s - 1], lambda i, s=s: hid.at[s - 1, i],
        )
        for s in range(1, n)
    ]
    for s in range(1, n):
        hid[s - 1, slot] = piece_ref[s - 1]

    def add(d, total):
        give(d).wait()
        return total + mail[d].astype(F32)

    total = lax.fori_loop(1, nv, add, part_ref[v].astype(F32))
    buf[0] = total.astype(BF16)
    crossing = [across(buf.at[0], buf.at[s], s, v, g, n, 1, ysend, yrecv) for s in range(1, n)]
    for copy in crossing:
        copy.start()
    for wait in waits:
        wait()
    hid_ref[...] = hid[...]
    for copy in crossing:
        copy.wait()
    out_ref[...] = buf[...]


def front(pieces, parts, n, nv, members):
    shape = (n - 1, members) + pieces.shape[1:]
    block = (n,) + parts.shape[1:]
    return pl.pallas_call(
        functools.partial(front_kernel, n, nv, members),
        out_shape=(jax.ShapeDtypeStruct(shape, BF16), jax.ShapeDtypeStruct(block, BF16)),
        in_specs=[VMEM] * 2,
        out_specs=(VMEM, VMEM),
        scratch_shapes=[
            pltpu.VMEM(shape, BF16),
            pltpu.VMEM(parts.shape, BF16),
            pltpu.VMEM(block, BF16),
            pltpu.SemaphoreType.DMA((n,)),
            pltpu.SemaphoreType.DMA((n,)),
            pltpu.SemaphoreType.DMA((nv,)),
            pltpu.SemaphoreType.DMA((nv,)),
            pltpu.SemaphoreType.DMA((n - 1, members)),
            pltpu.SemaphoreType.DMA((n - 1, members)),
        ],
        compiler_params=pltpu.CompilerParams(
            collective_id=1, has_side_effects=True, vmem_limit_bytes=40 << 20
        ),
        cost_estimate=pl.CostEstimate(flops=25 * 10**9, bytes_accessed=10**6, transcendentals=0),
        name="front",
    )(pieces, parts)


def gather_kernel(nv, members, block_ref, after_ref, out_ref, buf, zsend, zrecv, send, recv):
    v, g = lax.axis_index("vocab"), lax.axis_index("grp")
    slot = lax.rem(v, members)
    base = v - slot
    levels = nv // members
    barrier = pltpu.get_barrier_semaphore()

    def far(d):
        return lax.rem(v + d * members, nv)

    def greet_far(d, carry):
        pl.semaphore_signal(barrier, inc=1, device_id=(far(d), g), device_id_type=MESH)
        return carry

    def greet_near(d, carry):
        pl.semaphore_signal(barrier, inc=1, device_id=(peer(v, d, members), g), device_id_type=MESH)
        return carry

    lax.fori_loop(1, levels, greet_far, 0)
    lax.fori_loop(1, members, greet_near, 0)
    pl.semaphore_wait(barrier, levels - 1 + members - 1)
    buf[v] = block_ref[...]

    def hop(d, landed):
        return pltpu.make_async_remote_copy(
            src_ref=buf.at[v],
            dst_ref=buf.at[landed],
            send_sem=zsend.at[d],
            recv_sem=zrecv.at[d],
            device_id=(far(d), g),
            device_id_type=MESH,
        )

    def origin(owner, d):
        return lax.rem(owner - d * members + nv, nv)

    def near(d, e, landed):
        return pltpu.make_async_remote_copy(
            src_ref=buf.at[origin(v, d)],
            dst_ref=buf.at[landed],
            send_sem=send.at[d, e],
            recv_sem=recv.at[d, e],
            device_id=(peer(v, e, members), g),
            device_id_type=MESH,
        )

    def start_far(d, carry):
        hop(d, v).start()
        return carry

    def forward(d, carry):
        def one(e, inner):
            near(d, e, origin(v, d)).start()
            return inner

        return lax.fori_loop(1, members, one, carry)

    def relay(d, carry):
        hop(d, origin(v, d)).wait_recv()
        return forward(d, carry)

    def drain(d, carry):
        def one(e, inner):
            owner = base + lax.rem(slot - e + members, members)
            near(d, e, origin(v, d)).wait_send()
            near(d, e, origin(owner, d)).wait_recv()
            return inner

        return lax.fori_loop(1, members, one, carry)

    def drain_far(d, carry):
        hop(d, v).wait_send()
        return carry

    lax.fori_loop(1, levels, start_far, 0)
    forward(0, 0)
    lax.fori_loop(1, levels, relay, 0)
    lax.fori_loop(0, levels, drain, 0)
    lax.fori_loop(1, levels, drain_far, 0)
    out_ref[...] = buf[...]


def gather(block, begun, nv, members):
    shape = (nv,) + block.shape
    levels = nv // members
    return pl.pallas_call(
        functools.partial(gather_kernel, nv, members),
        out_shape=jax.ShapeDtypeStruct(shape, BF16),
        in_specs=[VMEM] * 2,
        out_specs=VMEM,
        scratch_shapes=[
            pltpu.VMEM(shape, BF16),
            pltpu.SemaphoreType.DMA((levels,)),
            pltpu.SemaphoreType.DMA((levels,)),
            pltpu.SemaphoreType.DMA((levels, members)),
            pltpu.SemaphoreType.DMA((levels, members)),
        ],
        compiler_params=pltpu.CompilerParams(
            collective_id=2, has_side_effects=True, vmem_limit_bytes=40 << 20
        ),
        cost_estimate=pl.CostEstimate(flops=25 * 10**9, bytes_accessed=10**6, transcendentals=0),
        name="projection_gather",
    )(block, begun)


def merge(blocks):
    rows = []
    for c in range(4):
        m, s, w, p = (blocks[:, 4 * c + i, :] for i in range(4))
        top = jnp.max(m, axis=0, keepdims=True)
        scale = jnp.exp(m - top)
        rows += [
            top,
            jnp.sum(s * scale, axis=0, keepdims=True),
            jnp.sum(w * scale, axis=0, keepdims=True),
            jnp.sum(p, axis=0, keepdims=True),
        ]
    return rows


def final_kernel(n, nv, v_head, tail, tail_ref, head_ref, clus_ref, tgt_ref, flag_ref, out_ref,
                 mail, buf, ysend, yrecv, send, recv):
    v, g = lax.axis_index("vocab"), lax.axis_index("grp")
    greet(nv, n, nv, v, g)
    crossing = [
        across(tail_ref.at[s], mail.at[s], s, v, g, n, -1, ysend, yrecv) for s in range(1, n)
    ]
    for copy in crossing:
        copy.start()
    mail[0] = tail_ref[0]
    for copy in crossing:
        copy.wait()
    rows = merge(mail[...])
    buf[v] = jnp.concatenate(rows[:12] + [head_ref[...]], axis=0)
    spread(buf.at[v], buf, v, v, g, nv, send, recv, lambda i: buf.at[i])()
    rows = merge(buf[...])
    clus = clus_ref[...]
    targets = tgt_ref[...]
    head_max, head_sum, _, picked = rows[12:]
    for c in range(3):
        picked = picked + rows[4 * c + 3]
    top = jnp.maximum(head_max, jnp.max(clus, axis=0, keepdims=True))
    total = head_sum * jnp.exp(head_max - top) + jnp.sum(jnp.exp(clus - top), axis=0, keepdims=True)
    head_lse = top + jnp.log(total)
    term = jnp.zeros_like(head_lse)
    out = []
    for c in range(3):
        lse = rows[4 * c] + jnp.log(rows[4 * c + 1])
        mean = rows[4 * c + 2] / rows[4 * c + 1]
        out.append(flag_ref[c : c + 1, :] * (lse - mean))
        low = v_head + c * tail
        inside = jnp.logical_and(targets >= low, targets < low + tail)
        term = term + jnp.where(inside, clus[c : c + 1, :] - lse, 0.0)
    out_ref[...] = jnp.concatenate([picked + term - head_lse] + out, axis=0)


def finish(tails, head, clus, targets, flags, n, nv, v_head, tail):
    rows = head.shape[1]
    return pl.pallas_call(
        functools.partial(final_kernel, n, nv, v_head, tail),
        out_shape=jax.ShapeDtypeStruct((4, rows), F32),
        in_specs=[VMEM] * 5,
        out_specs=VMEM,
        scratch_shapes=[
            pltpu.VMEM((n, 16, rows), F32),
            pltpu.VMEM((nv, 16, rows), F32),
            pltpu.SemaphoreType.DMA((n,)),
            pltpu.SemaphoreType.DMA((n,)),
            pltpu.SemaphoreType.DMA((nv,)),
            pltpu.SemaphoreType.DMA((nv,)),
        ],
        compiler_params=pltpu.CompilerParams(
            collective_id=3, has_side_effects=True, vmem_limit_bytes=40 << 20
        ),
        name="totals",
    )(tails, head, clus, targets, flags)


def stats_kernel(parts, tile, last, *refs):
    xs, ws = refs[:parts], refs[parts : 2 * parts]
    tgt_ref, out_ref, acc = refs[2 * parts], refs[-2], refs[-1]
    step = pl.program_id(0)

    @pl.when(step == 0)
    def _():
        if len(refs) == 2 * parts + 4:
            acc[...] = refs[2 * parts + 1][...]
        else:
            acc[:, 0:1] = jnp.full((acc.shape[0], 1), -jnp.inf, F32)
            acc[:, 1:] = jnp.zeros((acc.shape[0], acc.shape[1] - 1), F32)

    logits = jnp.dot(xs[0][...], ws[0][...], preferred_element_type=F32)
    for x, w in zip(xs[1:], ws[1:]):
        logits += jnp.dot(x[...], w[...], preferred_element_type=F32)
    before = acc[:, 0:1]
    top = jnp.maximum(before, jnp.max(logits, axis=1, keepdims=True))
    scale = jnp.exp(before - top)
    expo = jnp.exp(logits - top)
    ids = lax.broadcasted_iota(jnp.int32, logits.shape, 1) + step * tile
    acc[:, 0:1] = top
    acc[:, 1:2] = acc[:, 1:2] * scale + jnp.sum(expo, axis=1, keepdims=True)
    acc[:, 2:3] = acc[:, 2:3] * scale + jnp.sum(expo * logits, axis=1, keepdims=True)
    acc[:, 3:4] += jnp.sum(jnp.where(ids == tgt_ref[...], logits, 0.0), axis=1, keepdims=True)

    @pl.when(step == pl.num_programs(0) - 1)
    def _():
        out_ref[...] = acc[...].T[:8] if last else acc[...]


def softmax_stats(xs, ws, targets, begun=(), last=True):
    rows, words = xs[0].shape[0], ws[0].shape[1]
    tile = 512 if words % 512 == 0 else words
    shape = (8, rows) if last else (rows, 128)
    return pl.pallas_call(
        functools.partial(stats_kernel, len(xs), tile, last),
        grid=(words // tile,),
        out_shape=jax.ShapeDtypeStruct(shape, F32),
        in_specs=[pl.BlockSpec(x.shape, lambda i: (0, 0)) for x in xs]
        + [pl.BlockSpec((w.shape[0], tile), lambda i: (0, i)) for w in ws]
        + [pl.BlockSpec((rows, 1), lambda i: (0, 0))]
        + [pl.BlockSpec((rows, 128), lambda i: (0, 0)) for _ in begun],
        out_specs=pl.BlockSpec(shape, lambda i: (0, 0)),
        scratch_shapes=[pltpu.VMEM((rows, 128), F32)],
        compiler_params=pltpu.CompilerParams(vmem_limit_bytes=40 << 20),
        cost_estimate=pl.CostEstimate(flops=rows, bytes_accessed=rows, transcendentals=0),
        name="softmax_stats",
    )(*xs, *ws, targets, *begun)


def shards(
    n, nv, hidden, head_weight, cluster_weight, proj_one, proj_two, proj_three,
    tail_one, tail_two, tail_three, targets, flags,
):
    v, g = lax.axis_index("vocab"), lax.axis_index("grp")
    rows, width = hidden.shape
    depth = width // n
    head_cols, tail_cols = head_weight.shape[1], tail_one.shape[1]
    v_head, tail = head_cols * nv, tail_cols * nv
    share = tail_cols // n
    members = 4 if nv % 4 == 0 else 1

    def shift(value, s):
        return lax.ppermute(value, "grp", [(i, (i + s) % n) for i in range(n)])

    def columns(value, index, size):
        return lax.dynamic_slice_in_dim(value, index * size, size, 1)

    def cut(value, index, first, size):
        return lax.dynamic_slice_in_dim(value, index * share + first, size, 1)

    def swapped(value, first, size, later=0):
        return [cut(value, g, first, size)] + [
            shift(cut(value, (g + s) % n, first + later, size), s) for s in range(1, n)
        ]

    def after(value):
        return (value[(0,) * value.ndim].astype(F32) > 1e30).astype(jnp.int32)

    quarter = rows // members
    mine = lax.dynamic_slice_in_dim(hidden, lax.rem(v, members) * quarter, quarter, 0)
    pieces = jnp.stack([shift(columns(mine, (g + s) % n, depth), s) for s in range(1, n)])

    split = tail_two.shape[0]
    small = [shift(jnp.concatenate([cut(t, (g + s) % n, 0, share) for t in (tail_two, tail_three)]), s) for s in range(1, n)]
    bounds = (0, share // 4, share // 4 * 3, share) if share % 512 == 0 else (0, share)
    spans = [(low, high - low) for low, high in zip(bounds, bounds[1:])]
    one = [swapped(tail_one, *spans[0])]
    away_targets = [shift(targets, s) for s in range(1, n)]

    features = columns(hidden, v, proj_one.shape[0])
    parts = jnp.concatenate(
        [jnp.dot(features, w, preferred_element_type=F32).astype(BF16) for w in (proj_one, proj_two, proj_three)],
        axis=1,
    )
    others, block = front(pieces, parts.reshape(nv, rows // nv, -1), n, nv, members)
    others = others.reshape(n - 1, rows, depth)

    later = after(block)
    for span in spans[1:2]:
        one.append(swapped(tail_one, *span, later))
    sent = [jnp.dot(others[s - 1], head_weight, preferred_element_type=F32).astype(BF16) for s in range(1, n)]
    arrived = [shift(sent[s - 1], -s) for s in range(1, n)]
    later = after(sent[0])
    for span in spans[2:]:
        one.append(swapped(tail_one, *span, later))
    own = jnp.dot(columns(hidden, g, depth), head_weight, preferred_element_type=F32)
    projected = gather(block, sent[0][:16, :128], nv, members)
    later = after(projected)
    two, three = (
        [cut(t, g, 0, share)] + [lax.dynamic_slice_in_dim(w, low + later, t.shape[0], 0) for w in small]
        for t, low in ((tail_two, 0), (tail_three, split))
    )
    all_targets = jnp.concatenate([targets] + [t + later for t in away_targets])
    projected = jnp.transpose(projected, (1, 0, 2, 3)).reshape(n * rows, -1)

    def ordered(value, weight):
        size = weight.shape[0]
        return [columns(value, (g - s + n) % n, size) for s in range(n)]

    p1, p2 = proj_one.shape[1], proj_two.shape[1]
    proj = (projected[:, :p1], projected[:, p1 : p1 + p2], projected[:, p1 + p2 :])
    relative = all_targets - v_head
    cluster = relative // tail
    local = relative - cluster * tail - (v * tail_cols + g * share)
    marks = [jnp.where(cluster == c, local, -1)[:, None] for c in range(3)]

    def joined(value, weights, mark):
        x = jnp.concatenate(ordered(value, weights[0]), axis=1)
        return softmax_stats([x], [jnp.concatenate(weights, axis=0)], mark)

    stats_two = joined(proj[1], two, marks[1])
    stats_three = joined(proj[2], three, marks[2])
    ones, begun = ordered(proj[0], tail_one), ()
    for (low, _), words in zip(spans[:-1], one[:-1]):
        begun = (softmax_stats(ones, words, marks[0] - low, begun, False),)
    stats_one = softmax_stats(ones, one[-1], marks[0] - spans[-1][0], begun)
    totals = jnp.concatenate([stats_one[:4], stats_two[:4], stats_three[:4], jnp.zeros((4, n * rows), F32)])
    totals = jnp.transpose(totals.reshape(16, n, rows), (1, 0, 2))

    logits = own
    for value in arrived:
        logits = logits + value.astype(F32)
    head_max = jnp.max(logits, axis=1)
    head_sum = jnp.sum(jnp.exp(logits - head_max[:, None]), axis=1)
    ids = v * head_cols + lax.broadcasted_iota(jnp.int32, logits.shape, 1)
    head_pick = jnp.sum(jnp.where(ids == targets[:, None], logits, 0.0), axis=1)
    head = jnp.stack([head_max, head_sum, jnp.zeros_like(head_sum), head_pick])
    clus = jnp.dot(hidden, cluster_weight, preferred_element_type=F32)

    out = finish(totals, head, clus.T, targets[None, :], flags.astype(F32).T, n, nv, v_head, tail)
    return out[0], out[1:].T


def solution(mesh):
    n, nv = mesh.shape["grp"], mesh.shape["vocab"]
    return jax.shard_map(
        functools.partial(shards, n, nv),
        mesh=mesh,
        in_specs=(
            P("grp", None),
            P("grp", "vocab"),
            P(),
            P("vocab", None),
            P("vocab", None),
            P("vocab", None),
            P("grp", "vocab"),
            P("grp", "vocab"),
            P("grp", "vocab"),
            P("grp"),
            P("grp", None),
        ),
        out_specs=(P("grp"), P("grp", None)),
        check_vma=False,
    )
```
